128 devices in a mesh: gx: 8 (over y, core), gy: 16 (over x, z).
Axes of the slice: x: 4, y: 4, z: 4, core: 2. Of those that a mesh axis runs over, the one named last changes fastest.
Arguments:
- load: float32 [8, 16, 2, 112, 512], P('gx', 'gy'), may hold values from -6 to 6
- schur_inv: bfloat16 [8, 16, 2048, 2048], P('gx', 'gy'), as said below
- schur: bfloat16 [8, 16, 2048, 2048], P('gx', 'gy'), as said below
- coupling: bfloat16 [8, 16, 2048, 192], P('gx', 'gy'), may hold values from -0.125 to 0.125
- pairing: int32 [8, 16, 2, 4], P('gx', 'gy'), may hold values from 0 to 3, each once within a row
- corner_rows: int32 [8, 16, 192], P('gx', 'gy'), may hold values from 0 to 12287, as said below
- coarse_inv: float32 [12288, 96], P(('gx', 'gy')), as said below
Outputs:
- multipliers: float32 [8, 16, 2, 112, 512], P('gx', 'gy')
- residual: float32 [8, 16, 2, 112, 512], P('gx', 'gy')
The draws below stay inside these ranges and needn't reach their ends.
Inputs may be any that keep to these rules, and one draw needn't show every extreme that they name: `schur_inv`: each subdomain's block is symmetric positive definite. `schur`: each subdomain's block is symmetric positive definite. `coarse_inv`: each block of 96 rows is symmetric positive definite. `corner_rows`: of one subdomain's 192 entries at most 3 lie in one block of 96 rows (rows b*96 to (b+1)*96 - 1); one block holds exactly 3 entries of every subdomain.
All inputs are finite; a program needn't handle non-finite values.
Results may differ from the reference program's by a relative error of at most 0.04.
Values may be sent and summed in bfloat16 or wider, within the bound.
A program may use at most 128 MiB of HBM per device.

```python
import math
import jax
import jax.numpy as jnp
from jax import lax

NI = 2048
BLK = 128
NCOR = 192
CB = 96
ITERS = 3
R = 112
F = 512
FB = 4
SX = 8
SY = 16
NC = 12288
CAP = 3


def spd_from(noise, diagonal, scales, order):
    off_part = (noise + jnp.swapaxes(noise, -1, -2)) * (0.4 / math.sqrt(2.0 * order))
    eye = jnp.eye(order, dtype=jnp.float32)
    matrix = off_part * (1.0 - eye) + eye * diagonal[..., :, None]
    roots = jnp.sqrt(scales)
    return matrix * roots[..., :, None] * roots[..., None, :]


def draw_schur_inv(key, part):
    key = jax.random.fold_in(key, 11)
    first, second, third = jax.random.split(key, 3)
    shape = (SX, SY, NI, NI)
    noise = jax.random.normal(first, shape, jnp.float32)
    scales = jnp.exp(jax.random.uniform(third, (SX, SY, NI), jnp.float32, math.log(0.5), math.log(2.0)))
    diagonal = jax.random.uniform(second, (SX, SY, NI), jnp.float32, 1.2, 2.4)
    return spd_from(noise, diagonal, scales, NI).astype(jnp.bfloat16)


def draw_schur(key, part):
    key = jax.random.fold_in(key, 12)
    first, second, third = jax.random.split(key, 3)
    shape = (SX, SY, NI, NI)
    noise = jax.random.normal(first, shape, jnp.float32)
    scales = jnp.exp(jax.random.uniform(third, (SX, SY, NI), jnp.float32, math.log(0.5), math.log(2.0)))
    diagonal = jax.random.uniform(second, (SX, SY, NI), jnp.float32, 1.2, 2.4)
    return spd_from(noise, diagonal, scales, NI).astype(jnp.bfloat16)


def draw_coarse_inv(key, part):
    key = jax.random.fold_in(key, 13)
    first, second, third = jax.random.split(key, 3)
    count = NC // CB
    shape = (count, CB, CB)
    noise = jax.random.normal(first, shape, jnp.float32)
    scales = jnp.exp(jax.random.uniform(third, (count, CB), jnp.float32, math.log(0.5), math.log(2.0)))
    diagonal = jax.random.uniform(second, (count, CB), jnp.float32, 1.2, 2.4)
    return spd_from(noise, diagonal, scales, CB).reshape(NC, CB)


def draw_corner_rows(key, part):
    key = jax.random.fold_in(key, 14)
    first, second, third, fourth = jax.random.split(key, 4)
    count = SX * SY
    common = jax.random.randint(first, (), 0, count).astype(jnp.int32)
    others = jax.vmap(lambda sub: jax.random.permutation(sub, count - 1))(jax.random.split(second, count))
    others = others.astype(jnp.int32)
    others = others + (others >= common).astype(jnp.int32)
    index = jnp.arange(NCOR, dtype=jnp.int32)
    column = jnp.maximum(index - CAP, 0) % (count - 1)
    owners = jnp.where(index[None, :] < CAP, common, jnp.take(others, column, axis=1))
    offsets = jax.random.randint(third, (count, NCOR), 0, CB).astype(jnp.int32)
    order = jax.vmap(lambda sub: jax.random.permutation(sub, NCOR))(jax.random.split(fourth, count))
    rows = jnp.take_along_axis(owners * CB + offsets, order.astype(jnp.int32), axis=1)
    return rows.reshape(SX, SY, NCOR).astype(jnp.int32)


def block_scale(own_key, dims, cuts, low, top_value):
    gain = 1.0
    for axis_at, blocks in cuts:
        draws = jax.random.uniform(jax.random.fold_in(jax.random.fold_in(own_key, 6), axis_at), (blocks,), jnp.float32, low / len(cuts), top_value / len(cuts))
        gain = gain * jnp.repeat(jnp.exp(draws), dims[axis_at] // blocks).reshape((-1,) + (1,) * (len(dims) - 1 - axis_at))
    return gain


def centred(stream_key, shape, scale, limit, cuts=(), held_as=jnp.bfloat16):
    result = jax.random.normal(stream_key, shape, jnp.float32) * scale
    if len(cuts) > 0:
        result = block_scale(stream_key, shape, cuts, -0.22, 0.18) * result
    return jnp.clip(result, min=-limit, max=limit).astype(held_as)


def setup_inputs(seed: int = 0) -> dict:
    arg_keys = jax.random.split(jax.random.key(seed), 8)
    return {
        "load": centred(arg_keys[0], (SX, SY, 2, R, F), 1.0, 6.0, ((0, 8), (1, 16)), jnp.float32),
        "schur_inv": draw_schur_inv(jax.random.fold_in(arg_keys[7], 71), 0),
        "schur": draw_schur(jax.random.fold_in(arg_keys[7], 71), 0),
        "coupling": centred(arg_keys[3], (SX, SY, NI, NCOR), NI ** -0.5, 0.125, ((0, 8), (1, 16))),
        "pairing": jax.vmap(lambda own: jax.random.permutation(own, FB))(jax.random.split(arg_keys[4], SX * SY * 2)).reshape((SX, SY, 2, FB)).astype(jnp.int32),
        "corner_rows": draw_corner_rows(jax.random.fold_in(arg_keys[7], 71), 0),
        "coarse_inv": draw_coarse_inv(jax.random.fold_in(arg_keys[7], 71), 0),
    }


HIGH = lax.Precision.HIGHEST


def face_mask():
    right_live = (jnp.arange(SX) < SX - 1).astype(jnp.float32)[:, None] * jnp.ones((1, SY), jnp.float32)
    upper_live = jnp.ones((SX, 1), jnp.float32) * (jnp.arange(SY) < SY - 1).astype(jnp.float32)[None, :]
    return jnp.stack([right_live, upper_live], axis=2)[:, :, :, None, None]


def make_table(pairing):
    return (pairing[..., :, None] == jnp.arange(FB, dtype=jnp.int32)[None, :]).astype(jnp.float32)


def assemble(field, table):
    right = field[:, :, 0]
    upper = field[:, :, 1]
    from_left = jnp.concatenate([jnp.zeros_like(right[:1]), right[:-1]], axis=0)
    from_below = jnp.concatenate([jnp.zeros_like(upper[:, :1]), upper[:, :-1]], axis=1)
    left = jnp.einsum('xyjk,xyrkb->xyrjb', table[:, :, 0], from_left.reshape(SX, SY, R, FB, BLK), precision=HIGH)
    lower = jnp.einsum('xyjk,xyrkb->xyrjb', table[:, :, 1], from_below.reshape(SX, SY, R, FB, BLK), precision=HIGH)
    left = left.reshape(SX, SY, R, F)
    lower = lower.reshape(SX, SY, R, F)
    return jnp.concatenate([-left, right, -lower, upper], axis=-1)


def jump(values, table, live):
    parts = values.reshape(SX, SY, R, 4, FB, BLK)
    back_left = jnp.einsum('xyjk,xyrjb->xyrkb', table[:, :, 0], parts[:, :, :, 0], precision=HIGH).reshape(SX, SY, R, F)
    back_low = jnp.einsum('xyjk,xyrjb->xyrkb', table[:, :, 1], parts[:, :, :, 2], precision=HIGH).reshape(SX, SY, R, F)
    from_right = jnp.concatenate([back_left[1:], jnp.zeros_like(back_left[:1])], axis=0)
    from_above = jnp.concatenate([back_low[:, 1:], jnp.zeros_like(back_low[:, :1])], axis=1)
    out = jnp.stack([values[..., F:2 * F] - from_right, values[..., 3 * F:] - from_above], axis=2)
    return out * live


def apply_each(mats, vecs):
    flat_m = mats.reshape((SX * SY,) + mats.shape[2:])
    flat_v = vecs.reshape((SX * SY,) + vecs.shape[2:])
    out = lax.map(lambda pair: jnp.dot(pair[1], pair[0], preferred_element_type=jnp.float32), (flat_m, flat_v))
    return out.reshape((SX, SY) + out.shape[1:])


def apply_back(mats, vecs):
    flat_m = mats.reshape((SX * SY,) + mats.shape[2:])
    flat_v = vecs.reshape((SX * SY,) + vecs.shape[2:])
    out = lax.map(lambda pair: jnp.dot(pair[1], pair[0].T, preferred_element_type=jnp.float32), (flat_m, flat_v))
    return out.reshape((SX, SY) + out.shape[1:])


def reference(load, schur_inv, schur, coupling, pairing, corner_rows, coarse_inv):
    live = face_mask()
    table = make_table(pairing)
    blocks = coarse_inv.reshape(NC // CB, CB, CB)
    flat_rows = corner_rows.reshape(-1)

    def operator(field):
        assembled = assemble(field, table).astype(jnp.bfloat16)
        values = apply_each(schur_inv, assembled)
        corner = apply_each(coupling, values.astype(jnp.bfloat16))
        spread = jnp.transpose(corner, (0, 1, 3, 2)).reshape(-1, R)
        summed = jnp.zeros((NC, R), jnp.float32).at[flat_rows].add(spread)
        solved = jnp.einsum('bjr,bjk->bkr', summed.reshape(NC // CB, CB, R), blocks, precision=HIGH).reshape(NC, R)
        picked = jnp.transpose(solved[flat_rows].reshape(SX, SY, NCOR, R), (0, 1, 3, 2)).astype(jnp.bfloat16)
        lifted = apply_back(coupling, picked).astype(jnp.bfloat16)
        full_values = values + apply_each(schur_inv, lifted)
        return jump(full_values, table, live)

    def precond(field):
        assembled = (0.5 * assemble(field, table)).astype(jnp.bfloat16)
        return 0.5 * jump(apply_each(schur, assembled), table, live)

    def inner(first, second):
        return jnp.sum(first * second, axis=(0, 1, 2, 4))

    residual = load * live
    multipliers = jnp.zeros_like(residual)
    search = precond(residual)
    direction = search
    norm_now = inner(residual, search)
    for step in range(ITERS):
        image = operator(direction)
        alpha = norm_now / inner(direction, image)
        multipliers = multipliers + alpha[:, None] * direction
        residual = residual - alpha[:, None] * image
        if step + 1 < ITERS:
            search = precond(residual)
            norm_next = inner(residual, search)
            direction = search + (norm_next / norm_now)[:, None] * direction
            norm_now = norm_next
    return multipliers, residual
```

```python
import functools

import jax
import jax.numpy as jnp
from jax import lax
from jax.experimental import pallas as pl
from jax.experimental.pallas import tpu as pltpu
from jax.sharding import PartitionSpec as P

ITERS = 3
MESH = pl.DeviceIdType.MESH
BF = jnp.bfloat16
F32 = jnp.float32
LANES = 128
WIDTH = 4


def log2(value):
    return value.bit_length() - 1


def radices(nx, ny):
    return (nx // 2, 2, max(1, ny // 4), min(4, ny))


def offsets_far_first(rad):
    dy, dc, dx, dz = rad
    found = [
        (y, c, x, z) for y in range(dy) for c in range(dc) for x in range(dx) for z in range(dz)
    ]

    def hops(t):
        chips = sum(min(d, r - d) for d, r in ((t[0], dy), (t[2], dx), (t[3], dz)))
        return 2 * chips + t[1]

    return sorted(found[1:], key=hops, reverse=True)


def kernel(
    nx, ny,
    load_ref, inverse_hbm, stiff_hbm, couple_hbm, pair_ref, row_ref, col_ref, coarse_ref,
    mult_ref, res_ref,
    inverse, stiff, couple, lift, drop, solve, coarse_pad,
    resid, direc, image, prec, fresh, mult, weights, values,
    slots, sent0, got0, sent1, got1, sent2, got2, owned, square, *rest,
):
    halo_send = (rest[0:4], rest[4:8])
    halo_got = (rest[8:12], rest[12:16])
    load_sem, halo_ssem, halo_rsem, all_ssem, all_rsem = rest[16:21]
    rhs = load_ref.shape[1]
    face = load_ref.shape[2]
    groups = face // LANES
    corners = row_ref.shape[1]
    count = nx * ny
    rad = radices(nx, ny)
    order = offsets_far_first(rad)
    a, b = lax.axis_index("gx"), lax.axis_index("gy")
    my_y, my_c, my_x, my_z = a // 2, lax.rem(a, 2), b // rad[3], lax.rem(b, rad[3])

    def device(t, sign):
        y, c, x, z = (
            lax.rem(mine + sign * step + radix, radix)
            for mine, step, radix in zip((my_y, my_c, my_x, my_z), t, rad)
        )
        return (y * 2 + c, x * rad[3] + z)

    def place(t):
        return ((t[0] * rad[1] + t[1]) * rad[2] + t[2]) * rad[3] + t[3]

    copies = [
        pltpu.make_async_copy(source, target, load_sem.at[i])
        for i, (source, target) in enumerate(
            ((couple_hbm, couple), (inverse_hbm, inverse), (stiff_hbm, stiff))
        )
    ]
    for copy in copies:
        copy.start()

    barrier = pltpu.get_barrier_semaphore()
    for t in order:
        pl.semaphore_signal(barrier, inc=1, device_id=device(t, 1), device_id_type=MESH)

    right_live = (a < nx - 1).astype(F32)
    left_live = (a > 0).astype(F32)
    upper_live = (b < ny - 1).astype(F32)
    lower_live = (b > 0).astype(F32)
    neighbours = (
        (lax.rem(a + 1, nx), b),
        (lax.rem(a + nx - 1, nx), b),
        (a, lax.rem(b + 1, ny)),
        (a, lax.rem(b + ny - 1, ny)),
    )

    def halo_copy(which, way):
        return pltpu.make_async_remote_copy(
            src_ref=halo_send[which][way],
            dst_ref=halo_got[which][way],
            send_sem=halo_ssem.at[which, way],
            recv_sem=halo_rsem.at[which, way],
            device_id=neighbours[way],
            device_id_type=MESH,
        )

    def all_start(which, source, target, sign):
        for t in order:
            rows = pl.ds(place(t) * WIDTH, WIDTH)
            pltpu.make_async_remote_copy(
                src_ref=source.at[rows],
                dst_ref=target.at[rows],
                send_sem=all_ssem.at[which],
                recv_sem=all_rsem.at[which],
                device_id=device(t, sign),
                device_id_type=MESH,
            ).start()
        target[0:WIDTH] = source[0:WIDTH]

    def all_wait(which, source, target):
        rows = pl.ds(WIDTH, (count - 1) * WIDTH)
        pltpu.make_async_remote_copy(
            src_ref=source.at[rows],
            dst_ref=target.at[rows],
            send_sem=all_ssem.at[which],
            recv_sem=all_rsem.at[which],
            device_id=neighbours[0],
            device_id_type=MESH,
        ).wait()

    def slot_of(rows):
        block = (rows * 43691) >> 22
        z = block & (rad[3] - 1)
        x = (block >> log2(rad[3])) & (rad[2] - 1)
        gx = block >> log2(rad[2] * rad[3])
        c = gx & 1
        y = gx >> 1
        dy = (y - my_y + rad[0]) & (rad[0] - 1)
        dc = (c - my_c + 2) & 1
        dx = (x - my_x + rad[2]) & (rad[2] - 1)
        dz = (z - my_z + rad[3]) & (rad[3] - 1)
        return block, rows - block * 96, place((dy, dc, dx, dz)) * WIDTH

    block_row, offset_row, slot_row = slot_of(row_ref[...])
    block_col, offset_col, slot_col = slot_of(col_ref[...])
    at_col = lax.broadcasted_iota(jnp.int32, (corners, corners), 0)
    at_row = lax.broadcasted_iota(jnp.int32, (corners, corners), 1)
    same = block_row == block_col
    rank_col = jnp.sum((same & (at_row < at_col)).astype(F32), axis=1, keepdims=True)
    rank_row = jnp.sum((same & (at_col < at_row)).astype(F32), axis=0, keepdims=True)
    slot_col = slot_col + rank_col.astype(jnp.int32)
    slot_row = slot_row + rank_row.astype(jnp.int32)
    total = count * WIDTH
    hot = (slot_col == lax.broadcasted_iota(jnp.int32, (corners, total), 1)).astype(F32).astype(BF)
    hot_t = slot_row == lax.broadcasted_iota(jnp.int32, (total, corners), 0)
    offset = jnp.sum(
        jnp.where(hot_t, offset_row.astype(F32) - 200.0, 0.0), axis=1, keepdims=True
    )
    sent0[...] = jnp.broadcast_to(offset + 200.0, (total, LANES))

    coarse_pad[...] = jnp.zeros_like(coarse_pad)
    coarse_pad[0 : coarse_ref.shape[0], 0 : coarse_ref.shape[1]] = coarse_ref[...]
    slots[...] = jnp.zeros_like(slots)
    square[...] = jnp.zeros_like(square)
    for ref in (direc, image, mult, owned):
        ref[...] = jnp.zeros_like(ref)
    for k in range(groups):
        part = slice(k * LANES, (k + 1) * LANES)
        halo_send[0][0][k] = load_ref[0, :, part].astype(BF)
        halo_send[0][2][k] = load_ref[1, :, part].astype(BF)

    pl.semaphore_wait(barrier, count - 1)
    first = [halo_copy(0, 2), halo_copy(0, 0)]
    for copy in first:
        copy.start()
    all_start(0, sent0, got0, 1)

    copies[0].wait()
    copies[1].wait()
    product = jnp.dot(inverse[...], couple[...], preferred_element_type=F32).astype(BF)
    spread = jnp.dot(product, hot, preferred_element_type=F32)
    drop[...] = spread.astype(BF)
    for k in range(4 * groups):
        part = slice(k * LANES, (k + 1) * LANES)
        lift[:, part] = spread[part].T.astype(BF)

    def block(f, k):
        return slice((f * groups + k) * LANES, (f * groups + k + 1) * LANES)

    def put_resid(f, k, value):
        resid[:, block(f, k)] = value
        weights[:, block(f, k)] = (0.5 * value).astype(BF)

    for copy in first:
        copy.wait()
    for k in range(groups):
        part = slice(k * LANES, (k + 1) * LANES)
        put_resid(1, k, load_ref[0, :, part] * right_live)
        put_resid(3, k, load_ref[1, :, part] * upper_live)
        put_resid(0, k, -halo_got[0][0][pair_ref[0, k]].astype(F32) * left_live)
        put_resid(2, k, -halo_got[0][2][pair_ref[1, k]].astype(F32) * lower_live)

    all_wait(0, sent0, got0)
    lane = lax.broadcasted_iota(jnp.int32, (total, LANES), 1).astype(F32)
    pick = (got0[...] == lane).astype(F32).astype(BF)
    wide = jnp.dot(pick, coarse_pad[...].astype(BF), preferred_element_type=F32).astype(BF)
    solve[...] = lax.dot_general(
        wide, pick, (((1,), (1,)), ((), ())), preferred_element_type=F32
    ).astype(BF)
    copies[2].wait()

    inverse_pair = [
        [
            sum(j * (pair_ref[side, j] == k).astype(jnp.int32) for j in range(groups))
            for k in range(groups)
        ]
        for side in range(2)
    ]

    def send_faces(which, side):
        low, high = (0, 1) if side == 0 else (2, 3)
        for k in range(groups):
            halo_send[which][high - 1][k] = values[high * groups + k].astype(BF)
            halo_send[which][high][k] = values[low * groups + inverse_pair[side][k]].astype(BF)
        sent = [halo_copy(which, high - 1), halo_copy(which, high)]
        for copy in sent:
            copy.start()
        return sent

    def jumped(which, f, k):
        own = values[f * groups + k]
        if f == 0:
            return (own - halo_got[which][0][pair_ref[0, k]].astype(F32)) * left_live
        if f == 1:
            return (own - halo_got[which][1][k].astype(F32)) * right_live
        if f == 2:
            return (own - halo_got[which][2][pair_ref[1, k]].astype(F32)) * lower_live
        return (own - halo_got[which][3][k].astype(F32)) * upper_live

    lane_slot = lax.broadcasted_iota(jnp.int32, (rhs, total), 1) & (WIDTH - 1)
    row_slot = lax.broadcasted_iota(jnp.int32, (total, LANES), 0) & (WIDTH - 1)
    real = lax.broadcasted_iota(jnp.int32, (1, LANES), 1) < rhs

    def as_row(value):
        square[0:rhs, :] = value
        return jnp.sum(square[...].T, axis=0, keepdims=True)

    def as_columns(row):
        return jnp.broadcast_to(row, (LANES, LANES)).T[0:rhs]

    def dots_row(received):
        return jnp.sum(jnp.where(row_slot == WIDTH - 1, received, 0.0), axis=0, keepdims=True)

    def iteration(step, carry):
        norm_before, local_before = carry
        later = (step > 0).astype(F32)

        sent = []
        norm_part = jnp.zeros((rhs, LANES), F32)
        for side in (1, 0):
            for f in ((2, 3), (0, 1))[1 - side]:
                out = jnp.dot(
                    weights[...], stiff[:, f * face : (f + 1) * face], preferred_element_type=F32
                )
                for k in range(groups):
                    values[f * groups + k] = out[:, k * LANES : (k + 1) * LANES]
            sent += send_faces(1, side)
        for f in range(4):
            for k in range(groups):
                norm_part = norm_part + resid[:, block(f, k)] * values[f * groups + k]
        norm_col = 0.5 * jnp.sum(norm_part, axis=1, keepdims=True)
        for copy in sent:
            copy.wait()
        for f in range(4):
            for k in range(groups):
                z = 0.5 * jumped(1, f, k)
                prec[:, block(f, k)] = z
                weights[:, block(f, k)] = z.astype(BF)

        spread_out = jnp.dot(weights[...], drop[...], preferred_element_type=F32)
        slots[0:rhs, :] = jnp.where(lane_slot == WIDTH - 1, norm_col, spread_out)
        sent1[...] = slots[...].T
        all_start(1, sent1, got1, 1)

        part_new = jnp.zeros((rhs, LANES), F32)
        part_mix = jnp.zeros((rhs, LANES), F32)
        for f in range(4):
            out = jnp.dot(
                weights[...], inverse[:, f * face : (f + 1) * face], preferred_element_type=F32
            )
            for k in range(groups):
                at = block(f, k)
                v = out[:, k * LANES : (k + 1) * LANES]
                fresh[:, at] = v
                part_new = part_new + prec[:, at] * v
                part_mix = part_mix + (prec[:, at] * image[:, at] + direc[:, at] * v)
        dot_new = as_row(part_new)
        dot_mix = as_row(part_mix)

        all_wait(1, sent1, got1)
        received = got1[...]
        norm = dots_row(received)
        beta = jnp.where(real, norm / norm_before, 0.0) * later
        owned[...] = received + beta * owned[...]
        sums = owned[...]
        solved = jnp.dot(solve[...], sums.astype(BF), preferred_element_type=F32)
        local = dot_new + beta * (dot_mix + beta * local_before)
        energy = local + jnp.sum(sums * solved, axis=0, keepdims=True)
        sent2[...] = jnp.where(row_slot == WIDTH - 1, energy, solved)
        all_start(2, sent2, got2, -1)

        beta_cols = as_columns(beta)
        for k in range(4 * groups):
            at = slice(k * LANES, (k + 1) * LANES)
            direc[:, at] = prec[:, at] + beta_cols * direc[:, at]
            image[:, at] = fresh[:, at] + beta_cols * image[:, at]

        all_wait(2, sent2, got2)
        received = got2[...]
        alpha = jnp.where(real, norm / dots_row(received), 0.0)
        picked = received.T[0:rhs].astype(BF)
        sent = []
        for side in (1, 0):
            for f in ((2, 3), (0, 1))[1 - side]:
                at = slice(f * face, (f + 1) * face)
                out = image[:, at] + jnp.dot(picked, lift[:, at], preferred_element_type=F32)
                for k in range(groups):
                    values[f * groups + k] = out[:, k * LANES : (k + 1) * LANES]
            sent += send_faces(0, side)
        alpha_cols = as_columns(alpha)
        for k in range(groups):
            for i, f in enumerate((1, 3)):
                part = slice((i * groups + k) * LANES, (i * groups + k + 1) * LANES)
                mult[:, part] = mult[:, part] + alpha_cols * direc[:, block(f, k)]
        for copy in sent:
            copy.wait()
        for f in range(4):
            for k in range(groups):
                put_resid(f, k, resid[:, block(f, k)] - alpha_cols * jumped(0, f, k))
        return norm, local

    start = (jnp.ones((1, LANES), F32), jnp.zeros((1, LANES), F32))
    lax.fori_loop(0, ITERS, iteration, start)
    for i, f in enumerate((1, 3)):
        mult_ref[i] = mult[:, i * face : (i + 1) * face]
        res_ref[i] = resid[:, f * face : (f + 1) * face]


def on_device(nx, ny, load, schur_inv, schur, coupling, pairing, corner_rows, coarse_inv):
    field = load[0, 0]
    rhs, face = field.shape[1:]
    width = 4 * face
    groups = face // LANES
    corners = corner_rows.shape[-1]
    total = nx * ny * WIDTH
    vmem = pl.BlockSpec(memory_space=pltpu.VMEM)
    hbm = pl.BlockSpec(memory_space=pl.ANY)
    smem = pl.BlockSpec(memory_space=pltpu.SMEM)
    halo = pltpu.VMEM((groups, rhs, LANES), BF)
    chunk = pltpu.VMEM((total, LANES), F32)
    state = pltpu.VMEM((rhs, width), F32)
    dma = pltpu.SemaphoreType.DMA
    out = jax.ShapeDtypeStruct(field.shape, F32)
    mult, res = pl.pallas_call(
        functools.partial(kernel, nx, ny),
        out_shape=(out, out),
        in_specs=[vmem, hbm, hbm, hbm, smem, vmem, vmem, vmem],
        out_specs=(vmem, vmem),
        scratch_shapes=[
            pltpu.VMEM((width, width), BF),
            pltpu.VMEM((width, width), BF),
            pltpu.VMEM((width, corners), BF),
            pltpu.VMEM((total, width), BF),
            pltpu.VMEM((width, total), BF),
            pltpu.VMEM((total, total), BF),
            pltpu.VMEM((LANES, LANES), F32),
            state, state, state, state, state,
            pltpu.VMEM((rhs, 2 * face), F32),
            pltpu.VMEM((rhs, width), BF),
            pltpu.VMEM((4 * groups, rhs, LANES), F32),
            pltpu.VMEM((LANES, total), F32),
            chunk, chunk, chunk, chunk, chunk, chunk, chunk,
            pltpu.VMEM((LANES, LANES), F32),
            *([halo] * 16),
            dma((3,)), dma((2, 4)), dma((2, 4)), dma((3,)), dma((3,)),
        ],
        compiler_params=pltpu.CompilerParams(
            collective_id=0, has_side_effects=True, vmem_limit_bytes=58 * 2**20
        ),
        name="feti",
    )(
        field, schur_inv[0, 0], schur[0, 0], coupling[0, 0], pairing[0, 0],
        corner_rows[0], corner_rows[0, 0][:, None], coarse_inv,
    )
    return (mult[None, None], res[None, None])


def solution(mesh):
    placed = (
        P("gx", "gy", None, None, None),
        P("gx", "gy", None, None),
        P("gx", "gy", None, None),
        P("gx", "gy", None, None),
        P("gx", "gy", None, None),
        P("gx", "gy", None),
        P(("gx", "gy"), None),
    )
    return jax.shard_map(
        functools.partial(on_device, mesh.shape["gx"], mesh.shape["gy"]),
        mesh=mesh,
        in_specs=placed,
        out_specs=(P("gx", "gy", None, None, None), P("gx", "gy", None, None, None)),
        check_vma=False,
    )
```

```python
import functools

import jax
import jax.numpy as jnp
from jax import lax
from jax.experimental import pallas as pl
from jax.experimental.pallas import tpu as pltpu
from jax.sharding import PartitionSpec as P

ITERS = 3
MESH = pl.DeviceIdType.MESH
BF = jnp.bfloat16
F32 = jnp.float32
LANES = 128
WIDTH = 4


def log2(value):
    return value.bit_length() - 1


def radices(nx, ny):
    return (nx // 2, 2, max(1, ny // 4), min(4, ny))


def offsets_far_first(rad):
    dy, dc, dx, dz = rad
    found = [
        (y, c, x, z) for y in range(dy) for c in range(dc) for x in range(dx) for z in range(dz)
    ]

    def hops(t):
        chips = sum(min(d, r - d) for d, r in ((t[0], dy), (t[2], dx), (t[3], dz)))
        return 2 * chips + t[1]

    return sorted(found[1:], key=hops, reverse=True)


def kernel(
    nx, ny,
    load_ref, inverse_hbm, stiff_hbm, couple_hbm, pair_ref, row_ref, coarse_ref,
    mult_ref, res_ref,
    inverse, stiff, couple, drop, solve, gather, coarse_pad,
    resid, direc, image, wave, whole, prec, mult, weights, values, norm_part,
    wide_row, slots, sent0, got0, sent1, got1, sent2, got2, owned, square, corner_mine, face_low, *rest,
):
    halo_send = (rest[0:4], rest[4:8])
    halo_got = (rest[8:12], rest[12:16])
    face_send, face_got = rest[16:20], rest[20:24]
    lift, corner_got = rest[24:28], rest[28:32]
    load_sem, halo_ssem, halo_rsem, all_ssem, all_rsem = rest[32:37]
    face_ssem, face_rsem, corner_ssem, corner_rsem = rest[37:41]
    rhs = load_ref.shape[1]
    face = load_ref.shape[2]
    groups = face // LANES
    corners = row_ref.shape[1]
    held = corner_mine.shape[1]
    count = nx * ny
    total = count * WIDTH
    rad = radices(nx, ny)
    order = offsets_far_first(rad)
    a, b = lax.axis_index("gx"), lax.axis_index("gy")
    my_y, my_c, my_x, my_z = a // 2, lax.rem(a, 2), b // rad[3], lax.rem(b, rad[3])

    def device(t, sign):
        y, c, x, z = (
            lax.rem(mine + sign * step + radix, radix)
            for mine, step, radix in zip((my_y, my_c, my_x, my_z), t, rad)
        )
        return (y * 2 + c, x * rad[3] + z)

    def place(t):
        return ((t[0] * rad[1] + t[1]) * rad[2] + t[2]) * rad[3] + t[3]

    copies = [
        pltpu.make_async_copy(source, target, load_sem.at[i])
        for i, (source, target) in enumerate(
            ((couple_hbm, couple), (inverse_hbm, inverse), (stiff_hbm, stiff))
        )
    ]
    for copy in copies:
        copy.start()

    barrier = pltpu.get_barrier_semaphore()
    for t in order:
        pl.semaphore_signal(barrier, inc=1, device_id=device(t, 1), device_id_type=MESH)

    live = (
        (a > 0).astype(F32),
        (a < nx - 1).astype(F32),
        (b > 0).astype(F32),
        (b < ny - 1).astype(F32),
    )
    neighbours = (
        (lax.rem(a + 1, nx), b),
        (lax.rem(a + nx - 1, nx), b),
        (a, lax.rem(b + 1, ny)),
        (a, lax.rem(b + ny - 1, ny)),
    )

    def halo_copy(which, way):
        return pltpu.make_async_remote_copy(
            src_ref=halo_send[which][way],
            dst_ref=halo_got[which][way],
            send_sem=halo_ssem.at[which, way],
            recv_sem=halo_rsem.at[which, way],
            device_id=neighbours[way],
            device_id_type=MESH,
        )

    def face_copy(way):
        return pltpu.make_async_remote_copy(
            src_ref=face_send[way],
            dst_ref=face_got[way],
            send_sem=face_ssem.at[way],
            recv_sem=face_rsem.at[way],
            device_id=neighbours[way],
            device_id_type=MESH,
        )

    def corner_copy(way):
        return pltpu.make_async_remote_copy(
            src_ref=corner_mine,
            dst_ref=corner_got[way],
            send_sem=corner_ssem.at[way],
            recv_sem=corner_rsem.at[way],
            device_id=neighbours[way],
            device_id_type=MESH,
        )

    def all_start(which, source, target, sign):
        for t in order:
            pltpu.make_async_remote_copy(
                src_ref=source.at[place(t)],
                dst_ref=target.at[place(t)],
                send_sem=all_ssem.at[which],
                recv_sem=all_rsem.at[which],
                device_id=device(t, sign),
                device_id_type=MESH,
            ).start()
        target[0] = source[0]

    def all_wait(which, source, target):
        others = pl.ds(1, count - 1)
        pltpu.make_async_remote_copy(
            src_ref=source.at[others],
            dst_ref=target.at[others],
            send_sem=all_ssem.at[which],
            recv_sem=all_rsem.at[which],
            device_id=neighbours[0],
            device_id_type=MESH,
        ).wait()

    def chunked(value):
        return value.reshape(count, WIDTH, LANES).astype(BF)

    def flat(ref):
        return ref[...].astype(F32).reshape(total, LANES)

    def part(k):
        return slice(k * LANES, (k + 1) * LANES)

    def block(f, k):
        return part(f * groups + k)

    def columns(f):
        return slice(f * face, (f + 1) * face)

    def half(side):
        return slice(2 * side * face, 2 * (side + 1) * face)

    inverse_pair = [
        [
            jnp.minimum(
                sum(j * (pair_ref[side, j] == k).astype(jnp.int32) for j in range(groups)),
                groups - 1,
            )
            for k in range(groups)
        ]
        for side in range(2)
    ]

    def met(f, k):
        return pair_ref[f // 2, k] if f in (0, 2) else k

    def slot_of(rows):
        owner = (rows * 43691) >> 22
        z = owner & (rad[3] - 1)
        x = (owner >> log2(rad[3])) & (rad[2] - 1)
        gx = owner >> log2(rad[2] * rad[3])
        c = gx & 1
        y = gx >> 1
        dy = (y - my_y + rad[0]) & (rad[0] - 1)
        dc = (c - my_c + 2) & 1
        dx = (x - my_x + rad[2]) & (rad[2] - 1)
        dz = (z - my_z + rad[3]) & (rad[3] - 1)
        return owner, rows - owner * 96, place((dy, dc, dx, dz)) * WIDTH

    block_row, offset_row, slot_row = slot_of(row_ref[...])
    wide_row[...] = jnp.full_like(wide_row, -1.0)
    wide_row[:, 0:corners] = jnp.broadcast_to(block_row.astype(F32), (wide_row.shape[0], corners))
    across = wide_row[...]
    at_col = lax.broadcasted_iota(jnp.int32, across.shape, 0)
    at_row = lax.broadcasted_iota(jnp.int32, across.shape, 1)
    earlier = (across == across.T) & (at_col < at_row)
    rank_row = jnp.sum(earlier.astype(F32), axis=0, keepdims=True)
    slot_row = slot_row + rank_row[:, 0:corners].astype(jnp.int32)
    hot = slot_row == lax.broadcasted_iota(jnp.int32, (total, corners), 0)
    offset = jnp.sum(jnp.where(hot, offset_row.astype(F32) - 200.0, 0.0), axis=1, keepdims=True)
    sent0[...] = chunked(jnp.broadcast_to(offset + 200.0, (total, LANES)))
    hot = hot.astype(F32).astype(BF)
    gather[...] = jnp.zeros_like(gather)
    gather[:, 0:corners] = hot

    coarse_pad[...] = jnp.zeros_like(coarse_pad)
    coarse_pad[0 : coarse_ref.shape[0], 0 : coarse_ref.shape[1]] = coarse_ref[...]
    slots[...] = jnp.zeros_like(slots)
    square[...] = jnp.zeros_like(square)
    for ref in (direc, image, wave, mult, owned, *lift):
        ref[...] = jnp.zeros_like(ref)
    for k in range(groups):
        halo_send[0][0][k] = load_ref[0, :, part(k)].astype(BF)
        halo_send[0][2][k] = load_ref[1, :, part(k)].astype(BF)

    pl.semaphore_wait(barrier, count - 1)
    first = [halo_copy(0, 2), halo_copy(0, 0)]
    for copy in first:
        copy.start()
    all_start(0, sent0, got0, 1)

    copies[0].wait()
    copies[1].wait()
    product = jnp.dot(couple[...], inverse[...], preferred_element_type=F32)
    for side in (1, 0):
        low, high = 2 * side, 2 * side + 1
        for k in range(groups):
            face_send[high - 1][k] = product[:, block(high, k)].astype(BF)
            face_low[k] = product[:, block(low, k)]
        for k in range(groups):
            face_send[high][k] = face_low[inverse_pair[side][k]].astype(BF)
    for f in range(4):
        for k in range(groups):
            lift[f][0:corners, part(k)] = (product[:, block(f, k)] * live[f]).astype(BF)
    spread = jnp.dot(hot, product.astype(BF), preferred_element_type=F32)
    for k in range(4 * groups):
        drop[part(k), :] = spread[:, part(k)].T.astype(BF)

    def put_resid(f, k, value):
        resid[:, block(f, k)] = value
        weights[:, block(f, k)] = (0.5 * value).astype(BF)

    def stiff_half(side, f):
        return jnp.dot(
            weights[:, half(side)], stiff[half(side), columns(f)], preferred_element_type=F32
        )

    def stiff_first():
        for f in (2, 3, 0, 1):
            out = stiff_half(0, f)
            for k in range(groups):
                values[f * groups + k] = out[:, part(k)]

    def send_faces(which, side, ways=2):
        low, high = 2 * side, 2 * side + 1
        for k in range(groups):
            if ways == 2:
                halo_send[which][high - 1][k] = values[high * groups + k].astype(BF)
            halo_send[which][high][k] = values[low * groups + inverse_pair[side][k]].astype(BF)
        sent = [halo_copy(which, way) for way in (high - 1, high)[2 - ways :]]
        for copy in sent:
            copy.start()
        return sent

    def jumped(which, f, k):
        came = halo_got[which][f][met(f, k)].astype(F32)
        return (values[f * groups + k] - came) * live[f]

    lane_slot = lax.broadcasted_iota(jnp.int32, (rhs, total), 1) & (WIDTH - 1)
    row_slot = lax.broadcasted_iota(jnp.int32, (total, LANES), 0) & (WIDTH - 1)
    real = lax.broadcasted_iota(jnp.int32, (1, LANES), 1) < rhs

    def as_row(value):
        square[0:rhs, :] = value
        return jnp.sum(square[...].T, axis=0, keepdims=True)

    def as_columns(row):
        return jnp.broadcast_to(row, (LANES, LANES)).T[0:rhs]

    def dots_row(received):
        return jnp.sum(jnp.where(row_slot == WIDTH - 1, received, 0.0), axis=0, keepdims=True)

    def setup():
        all_wait(0, sent0, got0)
        lane = lax.broadcasted_iota(jnp.int32, (total, LANES), 1).astype(F32)
        pick = (flat(got0) == lane).astype(F32).astype(BF)
        wide = jnp.dot(pick, coarse_pad[...].astype(BF), preferred_element_type=F32).astype(BF)
        solve[...] = lax.dot_general(
            wide, pick, (((1,), (1,)), ((), ())), preferred_element_type=F32
        ).astype(BF)

    def setup_faces():
        for f in range(4):
            face_copy(f).wait()
            for k in range(groups):
                came = face_got[f][met(f, k)].astype(F32) * -live[f]
                lift[f][held : held + corners, part(k)] = came.astype(BF)

    def precondition(meanwhile=None):
        sent = [None, None]
        for side in (1, 0):
            for f in (2 * side, 2 * side + 1):
                out = stiff_half(1, f)
                for k in range(groups):
                    values[f * groups + k] = values[f * groups + k] + out[:, part(k)]
            sent[side] = send_faces(1, side)
        norm = jnp.zeros((rhs, LANES), F32)
        for f in range(4):
            for k in range(groups):
                norm = norm + resid[:, block(f, k)] * values[f * groups + k]
        norm_part[...] = norm
        if meanwhile is not None:
            meanwhile()
        for side in (0, 1):
            for copy in sent[side]:
                copy.wait()
            for f in (2 * side, 2 * side + 1):
                for k in range(groups):
                    z = 0.5 * jumped(1, f, k)
                    prec[:, block(f, k)] = z
                    weights[:, block(f, k)] = z.astype(BF)
            out = jnp.dot(weights[:, half(side)], drop[half(side), :], preferred_element_type=F32)
            if side == 0:
                slots[0:rhs, :] = out
        norm_col = 0.5 * jnp.sum(norm_part[...], axis=1, keepdims=True)
        slots[0:rhs, :] = jnp.where(lane_slot == WIDTH - 1, norm_col, slots[0:rhs, :] + out)
        sent1[...] = chunked(slots[...].T)
        all_start(1, sent1, got1, 1)

    def operate(carry, step, last):
        norm_before, local_before = carry
        later = 1.0 if last else (step > 0).astype(F32)
        part_new = jnp.zeros((rhs, LANES), F32)
        part_mix = jnp.zeros((rhs, LANES), F32)
        sent = []
        for side in (1, 0):
            for f in (2 * side, 2 * side + 1):
                out = jnp.dot(weights[...], inverse[:, columns(f)], preferred_element_type=F32)
                for k in range(groups):
                    at = block(f, k)
                    v = out[:, part(k)]
                    values[f * groups + k] = v
                    part_new = part_new + prec[:, at] * v
                    part_mix = part_mix + (prec[:, at] * image[:, at] + direc[:, at] * v)
            sent += send_faces(0, side, 1 if last else 2)
        dot_new = as_row(part_new)
        dot_mix = as_row(part_mix)

        all_wait(1, sent1, got1)
        received = flat(got1)
        norm = dots_row(received)
        beta = jnp.where(real, norm / norm_before, 0.0) * later
        owned[...] = received + beta * owned[...]
        sums = owned[...]
        solved = jnp.dot(solve[...], sums.astype(BF), preferred_element_type=F32)
        local = dot_new + beta * (dot_mix + beta * local_before)
        energy = local + jnp.sum(sums * solved, axis=0, keepdims=True)
        sent2[...] = chunked(jnp.where(row_slot == WIDTH - 1, energy, solved))
        all_start(2, sent2, got2, -1)

        beta_cols = as_columns(beta)
        for f in range(4):
            for k in range(groups):
                at = block(f, k)
                direc[:, at] = prec[:, at] + beta_cols * direc[:, at]
                image[:, at] = values[f * groups + k] + beta_cols * image[:, at]
        for copy in sent:
            copy.wait()
        if not last:
            pl.when(step == 0)(setup_faces)
        needed = (1, 3) if last else (0, 1, 2, 3)
        for f in needed:
            for k in range(groups):
                at = block(f, k)
                wave[:, at] = jumped(0, f, k) + beta_cols * wave[:, at]

        all_wait(2, sent2, got2)
        received = flat(got2)
        picked = received.T[0:rhs].astype(BF)
        mine = jnp.dot(picked, gather[...], preferred_element_type=F32).astype(BF)
        corner_mine[...] = mine
        sent = [[corner_copy(f) for f in needed if f // 2 == side] for side in range(2)]
        for copy in sent[1] + sent[0]:
            copy.start()
        alpha = jnp.where(real, norm / dots_row(received), 0.0)
        alpha_cols = as_columns(alpha)
        for i, f in enumerate((1, 3)):
            for k in range(groups):
                at = part(i * groups + k)
                mult[:, at] = mult[:, at] + alpha_cols * direc[:, block(f, k)]
        for f in needed:
            own = jnp.dot(mine, lift[f][0:held, :], preferred_element_type=F32)
            for k in range(groups):
                at = block(f, k)
                whole[:, at] = wave[:, at] + own[:, part(k)]
        for side in range(2):
            for copy in sent[side]:
                copy.wait()
            for f in needed:
                if f // 2 == side:
                    other = jnp.dot(
                        corner_got[f][...], lift[f][held:, :], preferred_element_type=F32
                    )
                    for k in range(groups):
                        at = block(f, k)
                        q = whole[:, at] + other[:, part(k)]
                        put_resid(f, k, resid[:, at] - alpha_cols * q)
            if side == 0 and not last:
                stiff_first()
        return norm, local

    first[1].wait()
    for k in range(groups):
        put_resid(1, k, load_ref[0, :, part(k)] * live[1])
        put_resid(0, k, -halo_got[0][0][met(0, k)].astype(F32) * live[0])
    copies[2].wait()
    stiff_first()
    first[0].wait()
    for k in range(groups):
        put_resid(3, k, load_ref[1, :, part(k)] * live[3])
        put_resid(2, k, -halo_got[0][2][met(2, k)].astype(F32) * live[2])
    precondition(setup)
    for f in (2, 3, 0, 1):
        face_copy(f).start()

    def iteration(step, carry):
        carry = operate(carry, step, False)
        precondition()
        return carry

    carry = (jnp.ones((1, LANES), F32), jnp.zeros((1, LANES), F32))
    carry = lax.fori_loop(0, ITERS - 1, iteration, carry)
    operate(carry, ITERS - 1, True)
    for i, f in enumerate((1, 3)):
        mult_ref[i] = mult[:, columns(i)]
        res_ref[i] = resid[:, columns(f)]


def passed_on(mult_in, res_in, mult_out, res_out, mult_held, res_held, in_sem, out_sem):
    parts = [
        (ref[0].at[i], ref[1].at[i], ref[2].at[i])
        for i in range(2)
        for ref in ((mult_in, mult_held, mult_out), (res_in, res_held, res_out))
    ]
    come = [pltpu.make_async_copy(p[0], p[1], in_sem.at[i]) for i, p in enumerate(parts)]
    go = [pltpu.make_async_copy(p[1], p[2], out_sem.at[i]) for i, p in enumerate(parts)]
    for copy in come:
        copy.start()
    for i in range(4):
        come[i].wait()
        go[i].start()
    for copy in go:
        copy.wait()


def on_device(nx, ny, load, schur_inv, schur, coupling, pairing, corner_rows, coarse_inv):
    field = load[0, 0]
    rhs, face = field.shape[1:]
    width = 4 * face
    groups = face // LANES
    corners = corner_rows.shape[-1]
    total = nx * ny * WIDTH
    vmem = pl.BlockSpec(memory_space=pltpu.VMEM)
    hbm = pl.BlockSpec(memory_space=pl.ANY)
    smem = pl.BlockSpec(memory_space=pltpu.SMEM)
    held = -(-corners // 256) * 256
    corner = pltpu.VMEM((rhs, held), BF)
    halo = pltpu.VMEM((groups, rhs, LANES), BF)
    chunk = pltpu.VMEM((nx * ny, WIDTH, LANES), BF)
    state = pltpu.VMEM((rhs, width), F32)
    dma = pltpu.SemaphoreType.DMA
    out = jax.ShapeDtypeStruct(field.shape, F32)
    mult, res = pl.pallas_call(
        functools.partial(kernel, nx, ny),
        out_shape=(out, out),
        in_specs=[vmem, hbm, hbm, hbm, smem, vmem, vmem],
        out_specs=(vmem, vmem),
        scratch_shapes=[
            pltpu.VMEM((width, width), BF),
            pltpu.VMEM((width, width), BF),
            pltpu.VMEM((corners, width), BF),
            pltpu.VMEM((width, total), BF),
            pltpu.VMEM((total, total), BF),
            pltpu.VMEM((total, held), BF),
            pltpu.VMEM((LANES, LANES), F32),
            state, state, state, state, state, state,
            pltpu.VMEM((rhs, 2 * face), F32),
            pltpu.VMEM((rhs, width), BF),
            pltpu.VMEM((4 * groups, rhs, LANES), F32),
            pltpu.VMEM((rhs, LANES), F32),
            pltpu.VMEM((held, held), F32),
            pltpu.VMEM((LANES, total), F32),
            chunk, chunk, chunk, chunk, chunk, chunk,
            pltpu.VMEM((total, LANES), F32),
            pltpu.VMEM((LANES, LANES), F32),
            corner,
            pltpu.VMEM((groups, corners, LANES), F32),
            *([halo] * 16),
            *([pltpu.VMEM((groups, corners, LANES), BF)] * 8),
            *([pltpu.VMEM((2 * held, face), BF)] * 4),
            *([corner] * 4),
            dma((3,)), dma((2, 4)), dma((2, 4)), dma((3,)), dma((3,)),
            dma((4,)), dma((4,)), dma((4,)), dma((4,)),
        ],
        compiler_params=pltpu.CompilerParams(
            collective_id=0, has_side_effects=True, vmem_limit_bytes=58 * 2**20
        ),
        name="feti",
    )(
        field, schur_inv[0, 0], schur[0, 0], coupling[0, 0].T, pairing[0, 0],
        corner_rows[0], coarse_inv,
    )
    mult, res = pl.pallas_call(
        passed_on,
        out_shape=(out, out),
        in_specs=[hbm, hbm],
        out_specs=(hbm, hbm),
        scratch_shapes=[pltpu.VMEM(field.shape, F32)] * 2 + [dma((4,)), dma((4,))],
        name="passed_on",
    )(mult, res)
    return (mult[None, None], res[None, None])


def solution(mesh):
    placed = (
        P("gx", "gy", None, None, None),
        P("gx", "gy", None, None),
        P("gx", "gy", None, None),
        P("gx", "gy", None, None),
        P("gx", "gy", None, None),
        P("gx", "gy", None),
        P(("gx", "gy"), None),
    )
    return jax.shard_map(
        functools.partial(on_device, mesh.shape["gx"], mesh.shape["gy"]),
        mesh=mesh,
        in_specs=placed,
        out_specs=(P("gx", "gy", None, None, None), P("gx", "gy", None, None, None)),
        check_vma=False,
    )
```

```python
import functools

import jax
import jax.numpy as jnp
from jax import lax
from jax.experimental import pallas as pl
from jax.experimental.pallas import tpu as pltpu
from jax.sharding import PartitionSpec as P

ITERS = 3
MESH = pl.DeviceIdType.MESH
BF = jnp.bfloat16
F32 = jnp.float32
LANES = 128
WIDTH = 4


def log2(value):
    return value.bit_length() - 1


def radices(nx, ny):
    return (nx // 2, 2, max(1, ny // 4), min(4, ny))


def offsets_far_first(rad):
    dy, dc, dx, dz = rad
    found = [
        (y, c, x, z) for y in range(dy) for c in range(dc) for x in range(dx) for z in range(dz)
    ]

    def hops(t):
        chips = sum(min(d, r - d) for d, r in ((t[0], dy), (t[2], dx), (t[3], dz)))
        return 2 * chips + t[1]

    return sorted(found[1:], key=hops, reverse=True)


def kernel(
    nx, ny,
    load_ref, inverse_hbm, stiff_hbm, couple_hbm, pair_ref, row_ref, coarse_ref,
    mult_ref, res_ref,
    inverse, stiff, couple, drop, solve, gather, coarse_pad,
    resid, direc, image, wave, prec, whole, mult, weights, values, norm_part,
    wide_row, slots, sent0, got0, sent1, got1, sent2, got2, owned, square, corner_mine, face_low, *rest,
):
    halo_send = (rest[0:4], rest[4:8])
    halo_got = (rest[8:12], rest[12:16])
    face_send, face_got = rest[16:20], rest[20:24]
    lift, corner_got = rest[24:28], rest[28:32]
    load_sem, halo_ssem, halo_rsem, all_ssem, all_rsem = rest[32:37]
    face_ssem, face_rsem, corner_ssem, corner_rsem, round_sem = rest[37:42]
    rhs = load_ref.shape[1]
    face = load_ref.shape[2]
    groups = face // LANES
    corners = row_ref.shape[1]
    held = corner_mine.shape[1]
    count = nx * ny
    total = count * WIDTH
    rad = radices(nx, ny)
    order = offsets_far_first(rad)
    a, b = lax.axis_index("gx"), lax.axis_index("gy")
    my_y, my_c, my_x, my_z = a // 2, lax.rem(a, 2), b // rad[3], lax.rem(b, rad[3])

    def device(t, sign):
        y, c, x, z = (
            lax.rem(mine + sign * step + radix, radix)
            for mine, step, radix in zip((my_y, my_c, my_x, my_z), t, rad)
        )
        return (y * 2 + c, x * rad[3] + z)

    def place(t):
        return ((t[0] * rad[1] + t[1]) * rad[2] + t[2]) * rad[3] + t[3]

    copies = [
        pltpu.make_async_copy(source, target, load_sem.at[i])
        for i, (source, target) in enumerate(
            ((couple_hbm, couple), (inverse_hbm, inverse), (stiff_hbm, stiff))
        )
    ]
    for copy in copies:
        copy.start()

    along_x = [(lax.rem(a + d, nx), b) for d in (1, nx - 1, *range(2, nx - 1))]
    along_y = [(a, lax.rem(b + d, ny)) for d in (1, ny - 1, *range(2, ny - 1))]
    along_x, along_y = along_x[: nx - 1], along_y[: ny - 1]
    barrier = pltpu.get_barrier_semaphore()
    for peer in along_y + along_x:
        pl.semaphore_signal(barrier, inc=1, device_id=peer, device_id_type=MESH)

    live = (
        (a > 0).astype(F32),
        (a < nx - 1).astype(F32),
        (b > 0).astype(F32),
        (b < ny - 1).astype(F32),
    )
    neighbours = (
        (lax.rem(a + 1, nx), b),
        (lax.rem(a + nx - 1, nx), b),
        (a, lax.rem(b + 1, ny)),
        (a, lax.rem(b + ny - 1, ny)),
    )

    def halo_copy(which, way):
        return pltpu.make_async_remote_copy(
            src_ref=halo_send[which][way],
            dst_ref=halo_got[which][way],
            send_sem=halo_ssem.at[which, way],
            recv_sem=halo_rsem.at[which, way],
            device_id=neighbours[way],
            device_id_type=MESH,
        )

    def face_copy(way):
        return pltpu.make_async_remote_copy(
            src_ref=face_send[way],
            dst_ref=face_got[way],
            send_sem=face_ssem.at[way],
            recv_sem=face_rsem.at[way],
            device_id=neighbours[way],
            device_id_type=MESH,
        )

    def corner_copy(way):
        return pltpu.make_async_remote_copy(
            src_ref=corner_mine,
            dst_ref=corner_got[way],
            send_sem=corner_ssem.at[way],
            recv_sem=corner_rsem.at[way],
            device_id=neighbours[way],
            device_id_type=MESH,
        )

    def all_start(which, source, target, sign):
        for t in order:
            pltpu.make_async_remote_copy(
                src_ref=source.at[place(t)],
                dst_ref=target.at[place(t)],
                send_sem=all_ssem.at[which],
                recv_sem=all_rsem.at[which],
                device_id=device(t, sign),
                device_id_type=MESH,
            ).start()
        target[0] = source[0]

    def all_wait(which, source, target):
        others = pl.ds(1, count - 1)
        pltpu.make_async_remote_copy(
            src_ref=source.at[others],
            dst_ref=target.at[others],
            send_sem=all_ssem.at[which],
            recv_sem=all_rsem.at[which],
            device_id=neighbours[0],
            device_id_type=MESH,
        ).wait()

    def chunked(value):
        return value.reshape(count, WIDTH, LANES).astype(BF)

    def flat(ref):
        return ref[...].astype(F32).reshape(total, LANES)

    def part(k):
        return slice(k * LANES, (k + 1) * LANES)

    def block(f, k):
        return part(f * groups + k)

    def columns(f):
        return slice(f * face, (f + 1) * face)

    def half(side):
        return slice(2 * side * face, 2 * (side + 1) * face)

    inverse_pair = [
        [
            jnp.minimum(
                sum(j * (pair_ref[side, j] == k).astype(jnp.int32) for j in range(groups)),
                groups - 1,
            )
            for k in range(groups)
        ]
        for side in range(2)
    ]

    def met(f, k):
        return pair_ref[f // 2, k] if f in (0, 2) else k

    for k in range(groups):
        halo_send[0][0][k] = load_ref[0, :, part(k)].astype(BF)
        halo_send[0][2][k] = load_ref[1, :, part(k)].astype(BF)

    pl.semaphore_wait(barrier, nx + ny - 2)
    first = [halo_copy(0, 2), halo_copy(0, 0)]
    for copy in first:
        copy.start()
    for peer in along_x:
        pl.semaphore_signal(round_sem, inc=1, device_id=peer, device_id_type=MESH)

    def slot_of(rows):
        owner = (rows * 43691) >> 22
        z = owner & (rad[3] - 1)
        x = (owner >> log2(rad[3])) & (rad[2] - 1)
        gx = owner >> log2(rad[2] * rad[3])
        c = gx & 1
        y = gx >> 1
        dy = (y - my_y + rad[0]) & (rad[0] - 1)
        dc = (c - my_c + 2) & 1
        dx = (x - my_x + rad[2]) & (rad[2] - 1)
        dz = (z - my_z + rad[3]) & (rad[3] - 1)
        return owner, rows - owner * 96, place((dy, dc, dx, dz)) * WIDTH

    block_row, offset_row, slot_row = slot_of(row_ref[...])
    wide_row[...] = jnp.full_like(wide_row, -1.0)
    wide_row[:, 0:corners] = jnp.broadcast_to(block_row.astype(F32), (wide_row.shape[0], corners))
    across = wide_row[...]
    at_col = lax.broadcasted_iota(jnp.int32, across.shape, 0)
    at_row = lax.broadcasted_iota(jnp.int32, across.shape, 1)
    earlier = (across == across.T) & (at_col < at_row)
    rank_row = jnp.sum(earlier.astype(F32), axis=0, keepdims=True)
    slot_row = slot_row + rank_row[:, 0:corners].astype(jnp.int32)
    hot = slot_row == lax.broadcasted_iota(jnp.int32, (total, corners), 0)
    offset = jnp.sum(jnp.where(hot, offset_row.astype(F32) - 200.0, 0.0), axis=1, keepdims=True)
    sent0[...] = chunked(jnp.broadcast_to(offset + 200.0, (total, LANES)))
    gather[...] = jnp.zeros_like(gather)
    gather[:, 0:corners] = hot.astype(F32).astype(BF)

    coarse_pad[...] = jnp.zeros_like(coarse_pad)
    coarse_pad[0 : coarse_ref.shape[0], 0 : coarse_ref.shape[1]] = coarse_ref[...]
    slots[...] = jnp.zeros_like(slots)
    square[...] = jnp.zeros_like(square)
    for ref in (direc, image, wave, mult, owned, *lift):
        ref[...] = jnp.zeros_like(ref)
    copies[0].wait()
    copies[1].wait()
    product = jnp.dot(couple[...], inverse[...], preferred_element_type=F32)
    for side in (1, 0):
        low, high = 2 * side, 2 * side + 1
        for k in range(groups):
            face_send[high - 1][k] = product[:, block(high, k)].astype(BF)
            face_low[k] = product[:, block(low, k)]
        for k in range(groups):
            face_send[high][k] = face_low[inverse_pair[side][k]].astype(BF)
    for f in range(4):
        for k in range(groups):
            lift[f][0:corners, part(k)] = (product[:, block(f, k)] * live[f]).astype(BF)
    whole[...] = jnp.zeros_like(whole)
    whole[0:corners, :] = product
    scatter = gather[...].astype(F32).T.astype(BF)
    for k in range(4 * groups):
        turned = whole[:, part(k)].T.astype(BF)
        drop[part(k), :] = jnp.dot(turned, scatter, preferred_element_type=F32).astype(BF)

    def put_resid(f, k, value):
        resid[:, block(f, k)] = value
        weights[:, block(f, k)] = (0.5 * value).astype(BF)

    def stiff_half(side, f):
        return jnp.dot(
            weights[:, half(side)], stiff[half(side), columns(f)], preferred_element_type=F32
        )

    def stiff_first():
        for f in (2, 3, 0, 1):
            out = stiff_half(0, f)
            for k in range(groups):
                values[f * groups + k] = out[:, part(k)]

    def send_faces(which, side, ways=2):
        low, high = 2 * side, 2 * side + 1
        for k in range(groups):
            if ways == 2:
                halo_send[which][high - 1][k] = values[high * groups + k].astype(BF)
            halo_send[which][high][k] = values[low * groups + inverse_pair[side][k]].astype(BF)
        sent = [halo_copy(which, way) for way in (high - 1, high)[2 - ways :]]
        for copy in sent:
            copy.start()
        return sent

    def jumped(which, f, k):
        came = halo_got[which][f][met(f, k)].astype(F32)
        return (values[f * groups + k] - came) * live[f]

    lane_slot = lax.broadcasted_iota(jnp.int32, (rhs, total), 1) & (WIDTH - 1)
    row_slot = lax.broadcasted_iota(jnp.int32, (total, LANES), 0) & (WIDTH - 1)
    real = lax.broadcasted_iota(jnp.int32, (1, LANES), 1) < rhs

    def as_row(value):
        square[0:rhs, :] = value
        return jnp.sum(square[...].T, axis=0, keepdims=True)

    def as_columns(row):
        return jnp.broadcast_to(row, (LANES, LANES)).T[0:rhs]

    def dots_row(received):
        return jnp.sum(jnp.where(row_slot == WIDTH - 1, received, 0.0), axis=0, keepdims=True)

    def tell_rows():
        pl.semaphore_wait(round_sem, nx - 1)
        all_start(0, sent0, got0, 1)

    def setup_owner():
        all_wait(0, sent0, got0)
        lane = lax.broadcasted_iota(jnp.int32, (total, LANES), 1).astype(F32)
        pick = (flat(got0) == lane).astype(F32).astype(BF)
        wide = jnp.dot(pick, coarse_pad[...].astype(BF), preferred_element_type=F32).astype(BF)
        solve[...] = lax.dot_general(
            wide, pick, (((1,), (1,)), ((), ())), preferred_element_type=F32
        ).astype(BF)

    def setup_faces():
        for f in range(4):
            face_copy(f).wait()
            for k in range(groups):
                came = face_got[f][met(f, k)].astype(F32) * -live[f]
                lift[f][held : held + corners, part(k)] = came.astype(BF)

    def precondition(meanwhile=None):
        sent = [None, None]
        for side in (1, 0):
            for f in (2 * side, 2 * side + 1):
                out = stiff_half(1, f)
                for k in range(groups):
                    values[f * groups + k] = values[f * groups + k] + out[:, part(k)]
            sent[side] = send_faces(1, side)
        norm = jnp.zeros((rhs, LANES), F32)
        for f in range(4):
            for k in range(groups):
                norm = norm + resid[:, block(f, k)] * values[f * groups + k]
        norm_part[...] = norm
        if meanwhile is not None:
            meanwhile()
        for side in (0, 1):
            for copy in sent[side]:
                copy.wait()
            for f in (2 * side, 2 * side + 1):
                for k in range(groups):
                    z = 0.5 * jumped(1, f, k)
                    prec[:, block(f, k)] = z
                    weights[:, block(f, k)] = z.astype(BF)
            out = jnp.dot(weights[:, half(side)], drop[half(side), :], preferred_element_type=F32)
            if side == 0:
                slots[0:rhs, :] = out
        norm_col = 0.5 * jnp.sum(norm_part[...], axis=1, keepdims=True)
        slots[0:rhs, :] = jnp.where(lane_slot == WIDTH - 1, norm_col, slots[0:rhs, :] + out)
        sent1[...] = chunked(slots[...].T)
        all_start(1, sent1, got1, 1)

    def operate(carry, step, last):
        norm_before, local_before = carry
        later = 1.0 if last else (step > 0).astype(F32)
        part_new = jnp.zeros((rhs, LANES), F32)
        part_mix = jnp.zeros((rhs, LANES), F32)
        sent = []
        for side in (1, 0):
            for f in (2 * side, 2 * side + 1):
                out = jnp.dot(weights[...], inverse[:, columns(f)], preferred_element_type=F32)
                for k in range(groups):
                    at = block(f, k)
                    v = out[:, part(k)]
                    values[f * groups + k] = v
                    part_new = part_new + prec[:, at] * v
                    part_mix = part_mix + (prec[:, at] * image[:, at] + direc[:, at] * v)
            sent += send_faces(0, side, 1 if last else 2)
        dot_new = as_row(part_new)
        dot_mix = as_row(part_mix)

        if not last:
            pl.when(step == 0)(setup_owner)
        all_wait(1, sent1, got1)
        received = flat(got1)
        norm = dots_row(received)
        beta = jnp.where(real, norm / norm_before, 0.0) * later
        owned[...] = received + beta * owned[...]
        sums = owned[...]
        solved = jnp.dot(solve[...], sums.astype(BF), preferred_element_type=F32)
        local = dot_new + beta * (dot_mix + beta * local_before)
        energy = local + jnp.sum(sums * solved, axis=0, keepdims=True)
        sent2[...] = chunked(jnp.where(row_slot == WIDTH - 1, energy, solved))
        all_start(2, sent2, got2, -1)

        beta_cols = as_columns(beta)
        for f in range(4):
            for k in range(groups):
                at = block(f, k)
                direc[:, at] = prec[:, at] + beta_cols * direc[:, at]
                image[:, at] = values[f * groups + k] + beta_cols * image[:, at]
        for copy in sent:
            copy.wait()
        if not last:
            pl.when(step == 0)(setup_faces)
        needed = (1, 3) if last else (0, 1, 2, 3)
        for f in needed:
            for k in range(groups):
                at = block(f, k)
                wave[:, at] = jumped(0, f, k) + beta_cols * wave[:, at]

        all_wait(2, sent2, got2)
        received = flat(got2)
        picked = received.T[0:rhs].astype(BF)
        mine = jnp.dot(picked, gather[...], preferred_element_type=F32).astype(BF)
        corner_mine[...] = mine
        sent = [[corner_copy(f) for f in needed if f // 2 == side] for side in range(2)]
        for copy in sent[1] + sent[0]:
            copy.start()
        alpha = jnp.where(real, norm / dots_row(received), 0.0)
        alpha_cols = as_columns(alpha)
        for i, f in enumerate((1, 3)):
            for k in range(groups):
                at = part(i * groups + k)
                mult[:, at] = mult[:, at] + alpha_cols * direc[:, block(f, k)]
        for f in needed:
            own = jnp.dot(mine, lift[f][0:held, :], preferred_element_type=F32)
            for k in range(groups):
                at = block(f, k)
                whole[0:rhs, at] = wave[:, at] + own[:, part(k)]
        for side in range(2):
            for copy in sent[side]:
                copy.wait()
            for f in needed:
                if f // 2 == side:
                    other = jnp.dot(
                        corner_got[f][...], lift[f][held:, :], preferred_element_type=F32
                    )
                    for k in range(groups):
                        at = block(f, k)
                        q = whole[0:rhs, at] + other[:, part(k)]
                        put_resid(f, k, resid[:, at] - alpha_cols * q)
            if side == 0 and not last:
                stiff_first()
        return norm, local

    first[1].wait()
    for k in range(groups):
        put_resid(1, k, load_ref[0, :, part(k)] * live[1])
        put_resid(0, k, -halo_got[0][0][met(0, k)].astype(F32) * live[0])
    copies[2].wait()
    stiff_first()
    first[0].wait()
    for k in range(groups):
        put_resid(3, k, load_ref[1, :, part(k)] * live[3])
        put_resid(2, k, -halo_got[0][2][met(2, k)].astype(F32) * live[2])
    precondition(tell_rows)
    for f in (2, 3, 0, 1):
        face_copy(f).start()

    def iteration(step, carry):
        carry = operate(carry, step, False)
        precondition()
        return carry

    carry = (jnp.ones((1, LANES), F32), jnp.zeros((1, LANES), F32))
    carry = lax.fori_loop(0, ITERS - 1, iteration, carry)
    operate(carry, ITERS - 1, True)
    for i, f in enumerate((1, 3)):
        mult_ref[i] = mult[:, columns(i)]
        res_ref[i] = resid[:, columns(f)]


def passed_on(mult_in, res_in, mult_out, res_out, mult_held, res_held, in_sem, out_sem):
    parts = [
        (ref[0].at[i], ref[1].at[i], ref[2].at[i])
        for i in range(2)
        for ref in ((mult_in, mult_held, mult_out), (res_in, res_held, res_out))
    ]
    come = [pltpu.make_async_copy(p[0], p[1], in_sem.at[i]) for i, p in enumerate(parts)]
    go = [pltpu.make_async_copy(p[1], p[2], out_sem.at[i]) for i, p in enumerate(parts)]
    for copy in come:
        copy.start()
    for i in range(4):
        come[i].wait()
        go[i].start()
    for copy in go:
        copy.wait()


def on_device(nx, ny, load, schur_inv, schur, coupling, pairing, corner_rows, coarse_inv):
    field = load[0, 0]
    rhs, face = field.shape[1:]
    width = 4 * face
    groups = face // LANES
    corners = corner_rows.shape[-1]
    total = nx * ny * WIDTH
    vmem = pl.BlockSpec(memory_space=pltpu.VMEM)
    hbm = pl.BlockSpec(memory_space=pl.ANY)
    smem = pl.BlockSpec(memory_space=pltpu.SMEM)
    held = -(-corners // 256) * 256
    corner = pltpu.VMEM((rhs, held), BF)
    halo = pltpu.VMEM((groups, rhs, LANES), BF)
    chunk = pltpu.VMEM((nx * ny, WIDTH, LANES), BF)
    state = pltpu.VMEM((rhs, width), F32)
    dma = pltpu.SemaphoreType.DMA
    out = jax.ShapeDtypeStruct(field.shape, F32)
    mult, res = pl.pallas_call(
        functools.partial(kernel, nx, ny),
        out_shape=(out, out),
        in_specs=[vmem, hbm, hbm, hbm, smem, vmem, vmem],
        out_specs=(vmem, vmem),
        scratch_shapes=[
            pltpu.VMEM((width, width), BF),
            pltpu.VMEM((width, width), BF),
            pltpu.VMEM((corners, width), BF),
            pltpu.VMEM((width, total), BF),
            pltpu.VMEM((total, total), BF),
            pltpu.VMEM((total, held), BF),
            pltpu.VMEM((LANES, LANES), F32),
            state, state, state, state, state,
            pltpu.VMEM((max(held, rhs), width), F32),
            pltpu.VMEM((rhs, 2 * face), F32),
            pltpu.VMEM((rhs, width), BF),
            pltpu.VMEM((4 * groups, rhs, LANES), F32),
            pltpu.VMEM((rhs, LANES), F32),
            pltpu.VMEM((held, held), F32),
            pltpu.VMEM((LANES, total), F32),
            chunk, chunk, chunk, chunk, chunk, chunk,
            pltpu.VMEM((total, LANES), F32),
            pltpu.VMEM((LANES, LANES), F32),
            corner,
            pltpu.VMEM((groups, corners, LANES), F32),
            *([halo] * 16),
            *([pltpu.VMEM((groups, corners, LANES), BF)] * 8),
            *([pltpu.VMEM((2 * held, face), BF)] * 4),
            *([corner] * 4),
            dma((3,)), dma((2, 4)), dma((2, 4)), dma((3,)), dma((3,)),
            dma((4,)), dma((4,)), dma((4,)), dma((4,)),
            pltpu.SemaphoreType.REGULAR,
        ],
        compiler_params=pltpu.CompilerParams(
            collective_id=0, has_side_effects=True, vmem_limit_bytes=58 * 2**20
        ),
        name="feti",
    )(
        field, schur_inv[0, 0], schur[0, 0], coupling[0, 0].T, pairing[0, 0],
        corner_rows[0], coarse_inv,
    )
    mult, res = pl.pallas_call(
        passed_on,
        out_shape=(out, out),
        in_specs=[hbm, hbm],
        out_specs=(hbm, hbm),
        scratch_shapes=[pltpu.VMEM(field.shape, F32)] * 2 + [dma((4,)), dma((4,))],
        name="passed_on",
    )(mult, res)
    return (mult[None, None], res[None, None])


def solution(mesh):
    placed = (
        P("gx", "gy", None, None, None),
        P("gx", "gy", None, None),
        P("gx", "gy", None, None),
        P("gx", "gy", None, None),
        P("gx", "gy", None, None),
        P("gx", "gy", None),
        P(("gx", "gy"), None),
    )
    return jax.shard_map(
        functools.partial(on_device, mesh.shape["gx"], mesh.shape["gy"]),
        mesh=mesh,
        in_specs=placed,
        out_specs=(P("gx", "gy", None, None, None), P("gx", "gy", None, None, None)),
        check_vma=False,
    )
```

```python
import functools

import jax
import jax.numpy as jnp
from jax import lax
from jax.experimental import pallas as pl
from jax.experimental.pallas import tpu as pltpu
from jax.sharding import PartitionSpec as P

ITERS = 3
MESH = pl.DeviceIdType.MESH
BF = jnp.bfloat16
F32 = jnp.float32
LANES = 128
WIDTH = 4


def log2(value):
    return value.bit_length() - 1


def radices(nx, ny):
    return (nx // 2, 2, max(1, ny // 4), min(4, ny))


def offsets_far_first(rad):
    dy, dc, dx, dz = rad
    found = [
        (y, c, x, z) for y in range(dy) for c in range(dc) for x in range(dx) for z in range(dz)
    ]

    def hops(t):
        chips = sum(min(d, r - d) for d, r in ((t[0], dy), (t[2], dx), (t[3], dz)))
        return 2 * chips + t[1]

    return sorted(found[1:], key=hops, reverse=True)


def kernel(
    nx, ny,
    load_ref, inverse_hbm, stiff_hbm, couple_hbm, pair_ref, row_ref, coarse_ref,
    mult_ref, res_ref,
    inverse, stiff, couple, drop, solve, gather, coarse_pad,
    resid, direc, image, wave, prec, whole, mult, weights, values, norm_part,
    wide_row, slots, sent0, got0, sent1, got1, sent2, got2, owned, square, corner_mine, face_low, *rest,
):
    halo_send = (rest[0:4], rest[4:8])
    halo_got = (rest[8:12], rest[12:16])
    face_send, face_got = rest[16:20], rest[20:24]
    lift, corner_got = rest[24:28], rest[28:32]
    load_sem, halo_ssem, halo_rsem, all_ssem, all_rsem = rest[32:37]
    face_ssem, face_rsem, corner_ssem, corner_rsem, round_sem = rest[37:42]
    rhs = load_ref.shape[1]
    face = load_ref.shape[2]
    groups = face // LANES
    corners = row_ref.shape[1]
    held = corner_mine.shape[1]
    count = nx * ny
    total = count * WIDTH
    rad = radices(nx, ny)
    order = offsets_far_first(rad)
    a, b = lax.axis_index("gx"), lax.axis_index("gy")
    my_y, my_c, my_x, my_z = a // 2, lax.rem(a, 2), b // rad[3], lax.rem(b, rad[3])

    def device(t, sign):
        y, c, x, z = (
            lax.rem(mine + sign * step + radix, radix)
            for mine, step, radix in zip((my_y, my_c, my_x, my_z), t, rad)
        )
        return (y * 2 + c, x * rad[3] + z)

    def place(t):
        return ((t[0] * rad[1] + t[1]) * rad[2] + t[2]) * rad[3] + t[3]

    copies = [
        pltpu.make_async_copy(source, target, load_sem.at[i])
        for i, (source, target) in enumerate(
            ((couple_hbm, couple), (inverse_hbm, inverse), (stiff_hbm, stiff))
        )
    ]
    for copy in copies:
        copy.start()

    along_x = [(lax.rem(a + d, nx), b) for d in (1, nx - 1, *range(2, nx - 1))]
    along_y = [(a, lax.rem(b + d, ny)) for d in (1, ny - 1, *range(2, ny - 1))]
    along_x, along_y = along_x[: nx - 1], along_y[: ny - 1]
    barrier = pltpu.get_barrier_semaphore()
    for peer in along_y + along_x:
        pl.semaphore_signal(barrier, inc=1, device_id=peer, device_id_type=MESH)

    live = (
        (a > 0).astype(F32),
        (a < nx - 1).astype(F32),
        (b > 0).astype(F32),
        (b < ny - 1).astype(F32),
    )
    neighbours = (
        (lax.rem(a + 1, nx), b),
        (lax.rem(a + nx - 1, nx), b),
        (a, lax.rem(b + 1, ny)),
        (a, lax.rem(b + ny - 1, ny)),
    )

    def halo_copy(which, way):
        return pltpu.make_async_remote_copy(
            src_ref=halo_send[which][way],
            dst_ref=halo_got[which][way],
            send_sem=halo_ssem.at[which, way],
            recv_sem=halo_rsem.at[which, way],
            device_id=neighbours[way],
            device_id_type=MESH,
        )

    def face_copy(way):
        return pltpu.make_async_remote_copy(
            src_ref=face_send[way],
            dst_ref=face_got[way],
            send_sem=face_ssem.at[way],
            recv_sem=face_rsem.at[way],
            device_id=neighbours[way],
            device_id_type=MESH,
        )

    def corner_copy(way):
        return pltpu.make_async_remote_copy(
            src_ref=corner_mine,
            dst_ref=corner_got[way],
            send_sem=corner_ssem.at[way],
            recv_sem=corner_rsem.at[way],
            device_id=neighbours[way],
            device_id_type=MESH,
        )

    def all_start(which, source, target, sign):
        for t in order:
            pltpu.make_async_remote_copy(
                src_ref=source.at[place(t)],
                dst_ref=target.at[place(t)],
                send_sem=all_ssem.at[which],
                recv_sem=all_rsem.at[which],
                device_id=device(t, sign),
                device_id_type=MESH,
            ).start()
        target[0] = source[0]

    def all_wait(which, source, target):
        others = pl.ds(1, count - 1)
        pltpu.make_async_remote_copy(
            src_ref=source.at[others],
            dst_ref=target.at[others],
            send_sem=all_ssem.at[which],
            recv_sem=all_rsem.at[which],
            device_id=neighbours[0],
            device_id_type=MESH,
        ).wait()

    def chunked(value):
        return value.reshape(count, WIDTH, LANES).astype(BF)

    def flat(ref):
        return ref[...].astype(F32).reshape(total, LANES)

    def part(k):
        return slice(k * LANES, (k + 1) * LANES)

    def block(f, k):
        return part(f * groups + k)

    def columns(f):
        return slice(f * face, (f + 1) * face)

    def half(side):
        return slice(2 * side * face, 2 * (side + 1) * face)

    inverse_pair = [
        [
            jnp.minimum(
                sum(j * (pair_ref[side, j] == k).astype(jnp.int32) for j in range(groups)),
                groups - 1,
            )
            for k in range(groups)
        ]
        for side in range(2)
    ]

    def met(f, k):
        return pair_ref[f // 2, k] if f in (0, 2) else k

    for k in range(groups):
        halo_send[0][0][k] = load_ref[0, :, part(k)].astype(BF)
        halo_send[0][2][k] = load_ref[1, :, part(k)].astype(BF)

    pl.semaphore_wait(barrier, nx + ny - 2)
    first = [halo_copy(0, 2), halo_copy(0, 0)]
    for copy in first:
        copy.start()
    for peer in along_x:
        pl.semaphore_signal(round_sem, inc=1, device_id=peer, device_id_type=MESH)

    def slot_of(rows):
        owner = (rows * 43691) >> 22
        z = owner & (rad[3] - 1)
        x = (owner >> log2(rad[3])) & (rad[2] - 1)
        gx = owner >> log2(rad[2] * rad[3])
        c = gx & 1
        y = gx >> 1
        dy = (y - my_y + rad[0]) & (rad[0] - 1)
        dc = (c - my_c + 2) & 1
        dx = (x - my_x + rad[2]) & (rad[2] - 1)
        dz = (z - my_z + rad[3]) & (rad[3] - 1)
        return owner, rows - owner * 96, place((dy, dc, dx, dz)) * WIDTH

    block_row, offset_row, slot_row = slot_of(row_ref[...])
    wide_row[...] = jnp.full_like(wide_row, -1.0)
    wide_row[:, 0:corners] = jnp.broadcast_to(block_row.astype(F32), (wide_row.shape[0], corners))
    across = wide_row[...]
    at_col = lax.broadcasted_iota(jnp.int32, across.shape, 0)
    at_row = lax.broadcasted_iota(jnp.int32, across.shape, 1)
    earlier = (across == across.T) & (at_col < at_row)
    rank_row = jnp.sum(earlier.astype(F32), axis=0, keepdims=True)
    slot_row = slot_row + rank_row[:, 0:corners].astype(jnp.int32)
    hot = slot_row == lax.broadcasted_iota(jnp.int32, (total, corners), 0)
    offset = jnp.sum(jnp.where(hot, offset_row.astype(F32) - 200.0, 0.0), axis=1, keepdims=True)
    sent0[...] = chunked(jnp.broadcast_to(offset + 200.0, (total, LANES)))
    gather[...] = jnp.zeros_like(gather)
    gather[:, 0:corners] = hot.astype(F32).astype(BF)

    coarse_pad[...] = jnp.zeros_like(coarse_pad)
    coarse_pad[0 : coarse_ref.shape[0], 0 : coarse_ref.shape[1]] = coarse_ref[...]
    slots[...] = jnp.zeros_like(slots)
    square[...] = jnp.zeros_like(square)
    for ref in (direc, image, wave, mult, owned, *lift):
        ref[...] = jnp.zeros_like(ref)
    copies[0].wait()
    copies[1].wait()
    product = jnp.dot(couple[...], inverse[...], preferred_element_type=F32)
    for side in (1, 0):
        low, high = 2 * side, 2 * side + 1
        for k in range(groups):
            face_send[high - 1][k] = product[:, block(high, k)].astype(BF)
            face_low[k] = product[:, block(low, k)]
        for k in range(groups):
            face_send[high][k] = face_low[inverse_pair[side][k]].astype(BF)
    for f in range(4):
        for k in range(groups):
            lift[f][0:corners, part(k)] = (product[:, block(f, k)] * live[f]).astype(BF)
    whole[...] = jnp.zeros_like(whole)
    whole[0:corners, :] = product
    pl.semaphore_wait(round_sem, nx - 1)
    all_start(0, sent0, got0, 1)

    def put_resid(f, k, value):
        resid[:, block(f, k)] = value
        weights[:, block(f, k)] = (0.5 * value).astype(BF)

    def stiff_half(side, f):
        return jnp.dot(
            weights[:, half(side)], stiff[half(side), columns(f)], preferred_element_type=F32
        )

    def stiff_first():
        for f in (2, 3, 0, 1):
            out = stiff_half(0, f)
            for k in range(groups):
                values[f * groups + k] = out[:, part(k)]

    def send_faces(which, side, ways=2):
        low, high = 2 * side, 2 * side + 1
        for k in range(groups):
            if ways == 2:
                halo_send[which][high - 1][k] = values[high * groups + k].astype(BF)
            halo_send[which][high][k] = values[low * groups + inverse_pair[side][k]].astype(BF)
        sent = [halo_copy(which, way) for way in (high - 1, high)[2 - ways :]]
        for copy in sent:
            copy.start()
        return sent

    def jumped(which, f, k):
        came = halo_got[which][f][met(f, k)].astype(F32)
        return (values[f * groups + k] - came) * live[f]

    lane_slot = lax.broadcasted_iota(jnp.int32, (rhs, total), 1) & (WIDTH - 1)
    row_slot = lax.broadcasted_iota(jnp.int32, (total, LANES), 0) & (WIDTH - 1)
    real = lax.broadcasted_iota(jnp.int32, (1, LANES), 1) < rhs

    def as_row(value):
        square[0:rhs, :] = value
        return jnp.sum(square[...].T, axis=0, keepdims=True)

    def as_columns(row):
        return jnp.broadcast_to(row, (LANES, LANES)).T[0:rhs]

    def dots_row(received):
        return jnp.sum(jnp.where(row_slot == WIDTH - 1, received, 0.0), axis=0, keepdims=True)

    def setup():
        scatter = gather[...].astype(F32).T.astype(BF)
        for k in range(4 * groups):
            turned = whole[:, part(k)].T.astype(BF)
            drop[part(k), :] = jnp.dot(turned, scatter, preferred_element_type=F32).astype(BF)
        all_wait(0, sent0, got0)
        lane = lax.broadcasted_iota(jnp.int32, (total, LANES), 1).astype(F32)
        pick = (flat(got0) == lane).astype(F32).astype(BF)
        wide = jnp.dot(pick, coarse_pad[...].astype(BF), preferred_element_type=F32).astype(BF)
        solve[...] = lax.dot_general(
            wide, pick, (((1,), (1,)), ((), ())), preferred_element_type=F32
        ).astype(BF)

    def setup_faces():
        for f in range(4):
            face_copy(f).wait()
            for k in range(groups):
                came = face_got[f][met(f, k)].astype(F32) * -live[f]
                lift[f][held : held + corners, part(k)] = came.astype(BF)

    def precondition(meanwhile=None):
        sent = [None, None]
        for side in (1, 0):
            for f in (2 * side, 2 * side + 1):
                out = stiff_half(1, f)
                for k in range(groups):
                    values[f * groups + k] = values[f * groups + k] + out[:, part(k)]
            sent[side] = send_faces(1, side)
        norm = jnp.zeros((rhs, LANES), F32)
        for f in range(4):
            for k in range(groups):
                norm = norm + resid[:, block(f, k)] * values[f * groups + k]
        norm_part[...] = norm
        if meanwhile is not None:
            meanwhile()
        for side in (0, 1):
            for copy in sent[side]:
                copy.wait()
            for f in (2 * side, 2 * side + 1):
                for k in range(groups):
                    z = 0.5 * jumped(1, f, k)
                    prec[:, block(f, k)] = z
                    weights[:, block(f, k)] = z.astype(BF)
            out = jnp.dot(weights[:, half(side)], drop[half(side), :], preferred_element_type=F32)
            if side == 0:
                slots[0:rhs, :] = out
        norm_col = 0.5 * jnp.sum(norm_part[...], axis=1, keepdims=True)
        slots[0:rhs, :] = jnp.where(lane_slot == WIDTH - 1, norm_col, slots[0:rhs, :] + out)
        sent1[...] = chunked(slots[...].T)
        all_start(1, sent1, got1, 1)

    def operate(carry, step, last):
        norm_before, local_before = carry
        later = 1.0 if last else (step > 0).astype(F32)
        part_new = jnp.zeros((rhs, LANES), F32)
        part_mix = jnp.zeros((rhs, LANES), F32)
        sent = []
        for side in (1, 0):
            for f in (2 * side, 2 * side + 1):
                out = jnp.dot(weights[...], inverse[:, columns(f)], preferred_element_type=F32)
                for k in range(groups):
                    at = block(f, k)
                    v = out[:, part(k)]
                    values[f * groups + k] = v
                    part_new = part_new + prec[:, at] * v
                    part_mix = part_mix + (prec[:, at] * image[:, at] + direc[:, at] * v)
            sent += send_faces(0, side, 1 if last else 2)
        dot_new = as_row(part_new)
        dot_mix = as_row(part_mix)

        all_wait(1, sent1, got1)
        received = flat(got1)
        norm = dots_row(received)
        beta = jnp.where(real, norm / norm_before, 0.0) * later
        owned[...] = received + beta * owned[...]
        sums = owned[...]
        solved = jnp.dot(solve[...], sums.astype(BF), preferred_element_type=F32)
        local = dot_new + beta * (dot_mix + beta * local_before)
        energy = local + jnp.sum(sums * solved, axis=0, keepdims=True)
        sent2[...] = chunked(jnp.where(row_slot == WIDTH - 1, energy, solved))
        all_start(2, sent2, got2, -1)

        beta_cols = as_columns(beta)
        for f in range(4):
            for k in range(groups):
                at = block(f, k)
                direc[:, at] = prec[:, at] + beta_cols * direc[:, at]
                image[:, at] = values[f * groups + k] + beta_cols * image[:, at]
        for copy in sent:
            copy.wait()
        if not last:
            pl.when(step == 0)(setup_faces)
        needed = (1, 3) if last else (0, 1, 2, 3)
        for f in needed:
            for k in range(groups):
                at = block(f, k)
                wave[:, at] = jumped(0, f, k) + beta_cols * wave[:, at]

        all_wait(2, sent2, got2)
        received = flat(got2)
        picked = received.T[0:rhs].astype(BF)
        mine = jnp.dot(picked, gather[...], preferred_element_type=F32).astype(BF)
        corner_mine[...] = mine
        sent = [[corner_copy(f) for f in needed if f // 2 == side] for side in range(2)]
        for copy in sent[1] + sent[0]:
            copy.start()
        alpha = jnp.where(real, norm / dots_row(received), 0.0)
        alpha_cols = as_columns(alpha)
        for i, f in enumerate((1, 3)):
            for k in range(groups):
                at = part(i * groups + k)
                value = mult[:, at] + alpha_cols * direc[:, block(f, k)]
                if last:
                    mult_ref[i, :, part(k)] = value
                else:
                    mult[:, at] = value
        for f in needed:
            own = jnp.dot(mine, lift[f][0:held, :], preferred_element_type=F32)
            for k in range(groups):
                at = block(f, k)
                whole[0:rhs, at] = wave[:, at] + own[:, part(k)]
        for side in range(2):
            for copy in sent[side]:
                copy.wait()
            for f in needed:
                if f // 2 == side:
                    other = jnp.dot(
                        corner_got[f][...], lift[f][held:, :], preferred_element_type=F32
                    )
                    for k in range(groups):
                        at = block(f, k)
                        q = whole[0:rhs, at] + other[:, part(k)]
                        value = resid[:, at] - alpha_cols * q
                        if last:
                            res_ref[side, :, part(k)] = value
                        else:
                            put_resid(f, k, value)
            if side == 0 and not last:
                stiff_first()
        return norm, local

    first[1].wait()
    for k in range(groups):
        put_resid(1, k, load_ref[0, :, part(k)] * live[1])
        put_resid(0, k, -halo_got[0][0][met(0, k)].astype(F32) * live[0])
    copies[2].wait()
    stiff_first()
    first[0].wait()
    for k in range(groups):
        put_resid(3, k, load_ref[1, :, part(k)] * live[3])
        put_resid(2, k, -halo_got[0][2][met(2, k)].astype(F32) * live[2])
    precondition(setup)
    for f in (2, 3, 0, 1):
        face_copy(f).start()

    def iteration(step, carry):
        carry = operate(carry, step, False)
        precondition()
        return carry

    carry = (jnp.ones((1, LANES), F32), jnp.zeros((1, LANES), F32))
    carry = lax.fori_loop(0, ITERS - 1, iteration, carry)
    operate(carry, ITERS - 1, True)


def passed_on(mult_in, res_in, mult_out, res_out, mult_held, res_held, in_sem, out_sem):
    parts = [
        (ref[0].at[i], ref[1].at[i], ref[2].at[i])
        for i in range(2)
        for ref in ((mult_in, mult_held, mult_out), (res_in, res_held, res_out))
    ]
    come = [pltpu.make_async_copy(p[0], p[1], in_sem.at[i]) for i, p in enumerate(parts)]
    go = [pltpu.make_async_copy(p[1], p[2], out_sem.at[i]) for i, p in enumerate(parts)]
    for copy in come:
        copy.start()
    for i in range(4):
        come[i].wait()
        go[i].start()
    for copy in go:
        copy.wait()


def on_device(nx, ny, load, schur_inv, schur, coupling, pairing, corner_rows, coarse_inv):
    field = load[0, 0]
    rhs, face = field.shape[1:]
    width = 4 * face
    groups = face // LANES
    corners = corner_rows.shape[-1]
    total = nx * ny * WIDTH
    vmem = pl.BlockSpec(memory_space=pltpu.VMEM)
    hbm = pl.BlockSpec(memory_space=pl.ANY)
    smem = pl.BlockSpec(memory_space=pltpu.SMEM)
    held = -(-corners // 256) * 256
    corner = pltpu.VMEM((rhs, held), BF)
    halo = pltpu.VMEM((groups, rhs, LANES), BF)
    chunk = pltpu.VMEM((nx * ny, WIDTH, LANES), BF)
    state = pltpu.VMEM((rhs, width), F32)
    dma = pltpu.SemaphoreType.DMA
    out = jax.ShapeDtypeStruct(field.shape, F32)
    mult, res = pl.pallas_call(
        functools.partial(kernel, nx, ny),
        out_shape=(out, out),
        in_specs=[vmem, hbm, hbm, hbm, smem, vmem, vmem],
        out_specs=(vmem, vmem),
        scratch_shapes=[
            pltpu.VMEM((width, width), BF),
            pltpu.VMEM((width, width), BF),
            pltpu.VMEM((corners, width), BF),
            pltpu.VMEM((width, total), BF),
            pltpu.VMEM((total, total), BF),
            pltpu.VMEM((total, held), BF),
            pltpu.VMEM((LANES, LANES), F32),
            state, state, state, state, state,
            pltpu.VMEM((max(held, rhs), width), F32),
            pltpu.VMEM((rhs, 2 * face), F32),
            pltpu.VMEM((rhs, width), BF),
            pltpu.VMEM((4 * groups, rhs, LANES), F32),
            pltpu.VMEM((rhs, LANES), F32),
            pltpu.VMEM((held, held), F32),
            pltpu.VMEM((LANES, total), F32),
            chunk, chunk, chunk, chunk, chunk, chunk,
            pltpu.VMEM((total, LANES), F32),
            pltpu.VMEM((LANES, LANES), F32),
            corner,
            pltpu.VMEM((groups, corners, LANES), F32),
            *([halo] * 16),
            *([pltpu.VMEM((groups, corners, LANES), BF)] * 8),
            *([pltpu.VMEM((2 * held, face), BF)] * 4),
            *([corner] * 4),
            dma((3,)), dma((2, 4)), dma((2, 4)), dma((3,)), dma((3,)),
            dma((4,)), dma((4,)), dma((4,)), dma((4,)),
            pltpu.SemaphoreType.REGULAR,
        ],
        compiler_params=pltpu.CompilerParams(
            collective_id=0, has_side_effects=True, vmem_limit_bytes=58 * 2**20
        ),
        name="feti",
    )(
        field, schur_inv[0, 0], schur[0, 0], coupling[0, 0].T, pairing[0, 0],
        corner_rows[0], coarse_inv,
    )
    mult, res = pl.pallas_call(
        passed_on,
        out_shape=(out, out),
        in_specs=[hbm, hbm],
        out_specs=(hbm, hbm),
        scratch_shapes=[pltpu.VMEM(field.shape, F32)] * 2 + [dma((4,)), dma((4,))],
        name="passed_on",
    )(mult, res)
    return (mult[None, None], res[None, None])


def solution(mesh):
    placed = (
        P("gx", "gy", None, None, None),
        P("gx", "gy", None, None),
        P("gx", "gy", None, None),
        P("gx", "gy", None, None),
        P("gx", "gy", None, None),
        P("gx", "gy", None),
        P(("gx", "gy"), None),
    )
    return jax.shard_map(
        functools.partial(on_device, mesh.shape["gx"], mesh.shape["gy"]),
        mesh=mesh,
        in_specs=placed,
        out_specs=(P("gx", "gy", None, None, None), P("gx", "gy", None, None, None)),
        check_vma=False,
    )
```
